32 devices in a mesh: groups: 2 (over x), dp: 16 (over z, y, core).
Axes of the slice: x: 2, y: 2, z: 4, core: 2. Of those that a mesh axis runs over, the one named last changes fastest.
Arguments:
- teacher_blocks: bfloat16 [24576, 2048], P(('groups', 'dp')), parts along dimension 0, may hold values from -9 to 9
- student_blocks: bfloat16 [24576, 2048], P(('groups', 'dp')), parts along dimension 0, may hold values from -9 to 9
- block_expert: int32 [192], P(('groups', 'dp')), parts along dimension 0, may hold values from 0 to 1
- block_count: int32 [32], P(('groups', 'dp')), parts along dimension 0, may hold values from 1 to 6, as said below
- gate_weight: bfloat16 [4, 2048, 384], P('groups'), parts along dimension 0, may hold values from -0.125 to 0.125
- up_weight: bfloat16 [4, 2048, 384], P('groups'), parts along dimension 0, may hold values from -0.125 to 0.125
Outputs:
- panels: float32 [1536, 768], P(('groups', 'dp')), parts along dimension 0
The draws below stay inside these ranges and needn't reach their ends.
There are 2 independent parts, one for each index of `groups`. The reference program is written for one: setup_inputs(seed, part) draws one part's arguments, and reference() takes and returns one part's arrays. A program takes and returns all parts, laid end to end along the dimension named above; each array names one. Nothing has to cross between parts.
Inputs may be any that keep to these rules, and one draw needn't show every extreme that they name: `block_count`: at least one device holds 6 live block pairs in every draw.
All inputs are finite; a program needn't handle non-finite values.
Results may differ from the reference program's by a relative error of at most 0.00092.
Values may be sent and summed in bfloat16 or wider, within the bound.
No kernel may reach another device: no remote copies, remote signals or barrier semaphores. Data moves between devices by JAX's collectives and lax.ppermute only.
A program may use at most 64 MiB of HBM per device.

```python
import jax
import jax.numpy as jnp
from jax import lax

D = 2048
F = 384
EXPERTS = 2
BLOCK = 128
MAXB = 6
SLOTS = 96
ROWS = 12288
N_DP = 16


def paired_normals(key):
    common = jax.random.normal(jax.random.fold_in(key, 11), (ROWS, D), jnp.float32)
    noise = jax.random.normal(jax.random.fold_in(key, 23), (ROWS, D), jnp.float32)
    return (common, noise)


def draw_teacher_blocks(key, part):
    common, noise = paired_normals(key)
    return common.astype(jnp.bfloat16)


def draw_student_blocks(key, part):
    common, noise = paired_normals(key)
    return (0.9 * common + 0.45 * noise).astype(jnp.bfloat16)


def draw_block_count(key, part):
    key_base = jax.random.fold_in(key, 5)
    key_full = jax.random.fold_in(key, 7)
    key_pick = jax.random.fold_in(key, 9)
    base = jax.random.randint(key_base, (N_DP,), 1, 3)
    filled = jax.random.randint(key_full, (N_DP,), 0, 8) == 0
    chosen = jax.random.randint(key_pick, (), 0, N_DP)
    filled = filled | (jnp.arange(N_DP) == chosen)
    return jnp.where(filled, MAXB, base).astype(jnp.int32)


def set_ends(drawn, key, least, largest):
    extent = drawn.shape
    index_at = [jax.random.randint(jax.random.fold_in(key, axis), (), 0, extent[axis]) for axis in range(len(extent))]
    drawn = drawn.at[tuple(index_at)].set(least)
    longest = extent.index(max(extent))
    index_at[longest] = (index_at[longest] + 1) % extent[longest]
    return drawn.at[tuple(index_at)].set(largest)


def scatter_about(rng, dims, deviation, limit, kind=jnp.bfloat16):
    result = jax.random.normal(rng, dims, jnp.float32) * deviation
    return jnp.minimum(jnp.maximum(result, -limit), limit).astype(kind)


def setup_inputs(seed: int = 0, part: int = 0) -> dict:
    seeds = jax.random.split(jax.random.key(seed), 7)
    own_keys = jax.random.split(jax.random.fold_in(seeds[6], part), 7)
    return {
        "teacher_blocks": draw_teacher_blocks(jax.random.fold_in(jax.random.fold_in(seeds[6], part), 71), part),
        "student_blocks": draw_student_blocks(jax.random.fold_in(jax.random.fold_in(seeds[6], part), 71), part),
        "block_expert": set_ends(jax.random.randint(own_keys[2], (SLOTS,), 0, EXPERTS), jax.random.fold_in(own_keys[2], 1), 0, EXPERTS - 1).astype(jnp.int32),
        "block_count": draw_block_count(jax.random.fold_in(jax.random.fold_in(seeds[6], part), 71), part),
        "gate_weight": scatter_about(own_keys[4], (EXPERTS, D, F), D ** -0.5, 0.125),
        "up_weight": scatter_about(own_keys[5], (EXPERTS, D, F), D ** -0.5, 0.125),
    }


def reference(teacher_blocks, student_blocks, block_expert, block_count, gate_weight, up_weight):
    scaling = 1.0 / (BLOCK * N_DP)
    device_ids = jnp.arange(N_DP, dtype=jnp.int32)

    def one_block(accum, flat_slot):
        device_id = flat_slot // MAXB
        slot_id = flat_slot % MAXB
        live_count = jnp.sum(jnp.where(device_ids == device_id, block_count, 0))

        def work(accum):
            rows_teacher = lax.dynamic_slice_in_dim(teacher_blocks, flat_slot * BLOCK, BLOCK, 0)
            rows_student = lax.dynamic_slice_in_dim(student_blocks, flat_slot * BLOCK, BLOCK, 0)
            expert = block_expert[flat_slot].astype(jnp.int32)
            gate_matrix = lax.dynamic_index_in_dim(gate_weight, expert, 0, keepdims=False)
            up_matrix = lax.dynamic_index_in_dim(up_weight, expert, 0, keepdims=False)
            stacked = jnp.concatenate([rows_student, rows_teacher], 0)
            gate_out = jnp.dot(stacked, gate_matrix, preferred_element_type=jnp.float32)
            up_out = jnp.dot(stacked, up_matrix, preferred_element_type=jnp.float32)
            hidden = (jax.nn.silu(gate_out) * up_out).astype(jnp.bfloat16)
            hidden_student = hidden[:BLOCK]
            hidden_teacher = hidden[BLOCK:]
            gram_term = jnp.dot(hidden_student.T, jnp.concatenate([hidden_student, hidden_teacher], 1), preferred_element_type=jnp.float32)
            current = lax.dynamic_slice_in_dim(accum, expert * F, F, 0)
            return lax.dynamic_update_slice_in_dim(accum, current + gram_term, expert * F, 0)

        return lax.cond(slot_id < live_count, work, lambda kept: kept, accum), None

    accum, _ = lax.scan(one_block, jnp.zeros((EXPERTS * F, 2 * F), jnp.float32), jnp.arange(SLOTS, dtype=jnp.int32))
    return accum * scaling
```

```python
import functools

import jax
import jax.numpy as jnp
from jax import lax
from jax.experimental import pallas as pl
from jax.experimental.pallas import tpu as pltpu
from jax.sharding import PartitionSpec as P

LANES = 128
TAIL = 16
TOP = 32700.0


def code_scale(exponent, mantissa):
    return (mantissa * (1.0 / 16384.0)) * jnp.exp2(exponent)


def write_codes(blocks, msg_ref):
    rows, width = blocks[0]().shape
    panels = width // LANES
    top = None
    for load in blocks:
        high = jnp.max(jnp.abs(load()), axis=0, keepdims=True)
        for c in range(panels):
            part = high[:, c * LANES : (c + 1) * LANES]
            top = part if top is None else jnp.maximum(top, part)
    exponent = jnp.clip(jnp.ceil(jnp.log2(jnp.maximum(top, 1e-30))), -100.0, 100.0)
    mantissa = jnp.ceil(top * jnp.exp2(-exponent) * 16384.0) + 1.0
    factor = TOP / code_scale(exponent, mantissa)
    for k, load in enumerate(blocks):
        for c in range(panels):
            part = load()[:, c * LANES : (c + 1) * LANES] * factor
            at = (k * panels + c) * rows
            msg_ref[at : at + rows, :] = jnp.round(part).astype(jnp.int32).astype(jnp.int16)
    line = lax.broadcasted_iota(jnp.int32, (TAIL, LANES), 0)
    tail = jnp.where(line == 0, exponent.astype(jnp.int32), mantissa.astype(jnp.int32))
    msg_ref[len(blocks) * panels * rows :, :] = tail.astype(jnp.int16)


def read_step(msg_ref):
    at = msg_ref.shape[0] - TAIL
    tail = msg_ref[at:, :].astype(jnp.int32).astype(jnp.float32)
    return code_scale(tail[0:1], tail[1:2]) * (1.0 / TOP)


def read_block(msg_ref, k, rows, panels, step):
    parts = []
    for c in range(panels):
        at = (k * panels + c) * rows
        parts.append(msg_ref[at : at + rows, :].astype(jnp.int32).astype(jnp.float32) * step)
    return jnp.concatenate(parts, axis=1)


def message_shape(count, rows, width):
    return jax.ShapeDtypeStruct((count * rows * (width // LANES) + TAIL, LANES), jnp.int16)


def block_offsets(orders):
    tables = []
    for order in orders:
        depth = len(order)
        tables.append(
            [
                sum(bit for i, bit in enumerate(order) if (k >> (depth - 1 - i)) & 1)
                for k in range(1 << depth)
            ]
        )
    return tables


def gram_kernel(
    plan, experts, count, teacher, student, gate, up, *rest
):
    if plan is None:
        acc, x, w, hid, masked, x_sem, w_sem = rest
    else:
        own, msg, x, w, hid, masked, acc, x_sem, w_sem = rest
    slots, both, _ = x.shape
    block = both // 2
    expert_total, _, two = w.shape
    width = two // 2
    live = count[0]

    def fresh(s):
        ok = s < live
        for t in range(s):
            ok = ok & (experts[t] != experts[s])
        return ok

    def x_copies(s):
        rows = pl.ds(s * block, block)
        return [
            pltpu.make_async_copy(student.at[rows], x.at[s, pl.ds(0, block)], x_sem.at[s, 0]),
            pltpu.make_async_copy(teacher.at[rows], x.at[s, pl.ds(block, block)], x_sem.at[s, 1]),
        ]

    def w_copies(e):
        return [
            pltpu.make_async_copy(gate.at[e], w.at[e, :, pl.ds(0, width)], w_sem.at[e, 0]),
            pltpu.make_async_copy(up.at[e], w.at[e, :, pl.ds(width, width)], w_sem.at[e, 1]),
        ]

    for s in range(slots):

        @pl.when(fresh(s))
        def _():
            for copy in w_copies(experts[s]):
                copy.start()

        @pl.when(s < live)
        def _():
            for copy in x_copies(s):
                copy.start()

    for s in range(slots):
        rows = pl.ds(s * block, block)

        @pl.when(fresh(s))
        def _():
            for copy in w_copies(experts[s]):
                copy.wait()

        @pl.when(s < live)
        def _():
            for copy in x_copies(s):
                copy.wait()
            expert = experts[s]
            out = jnp.dot(x[s], w[expert], preferred_element_type=jnp.float32)
            gate_out = out[:, :width]
            hidden = (gate_out / (1.0 + jnp.exp(-gate_out)) * out[:, width:]).astype(jnp.bfloat16)
            hid[rows, :width] = hidden[:block]
            hid[rows, width:] = hidden[block:]
            for e in range(expert_total):
                masked[e, rows] = jnp.where(expert == e, hidden[:block], jnp.zeros_like(hidden[:block]))

        @pl.when(s >= live)
        def _():
            hid[rows] = jnp.zeros((block, two), jnp.bfloat16)
            for e in range(expert_total):
                masked[e, rows] = jnp.zeros((block, width), jnp.bfloat16)

    for e in range(expert_total):
        gram = lax.dot_general(
            masked[e], hid[...], (((0,), (0,)), ((), ())), preferred_element_type=jnp.float32
        )
        if plan is None:
            acc[e * width : (e + 1) * width] = gram
        else:
            rows = acc.shape[1]
            per = width // rows
            acc[e * per : (e + 1) * per] = gram.reshape(per, rows, two)

    if plan is not None:
        me = lax.axis_index("dp")
        core = lax.rem(me, 2)
        chip = me // 2
        tables = block_offsets(plan)
        loads = []
        for k in range(len(tables[0])):
            mine = jnp.where(core == 0, tables[0][k], tables[1][k])
            theirs = jnp.where(core == 0, tables[1][k], tables[0][k])
            own[k] = acc[2 * (chip ^ mine) + core]
            there = 2 * (chip ^ theirs) + (1 - core)
            loads.append(lambda there=there: acc[there])
        write_codes(loads, msg)


def grams(teacher, student, experts, count, gate, up, ranks, plan):
    slots = experts.shape[0]
    block = teacher.shape[0] // slots
    depth = teacher.shape[1]
    expert_total, _, width = gate.shape
    two = 2 * width
    rows = expert_total * width // ranks
    scratch = [
        pltpu.VMEM((slots, 2 * block, depth), jnp.bfloat16),
        pltpu.VMEM((expert_total, depth, two), jnp.bfloat16),
        pltpu.VMEM((slots * block, two), jnp.bfloat16),
        pltpu.VMEM((expert_total, slots * block, width), jnp.bfloat16),
    ]
    sems = [pltpu.SemaphoreType.DMA((slots, 2)), pltpu.SemaphoreType.DMA((expert_total, 2))]
    if plan is None:
        out_shape = jax.ShapeDtypeStruct((expert_total * width, two), jnp.float32)
    else:
        scratch.append(pltpu.VMEM((ranks, rows, two), jnp.float32))
        out_shape = (
            jax.ShapeDtypeStruct((ranks // 2, rows, two), jnp.float32),
            message_shape(ranks // 2, rows, two),
        )
    smem = pl.BlockSpec(memory_space=pltpu.SMEM)
    hbm = pl.BlockSpec(memory_space=pl.ANY)
    return pl.pallas_call(
        functools.partial(gram_kernel, plan),
        out_shape=out_shape,
        in_specs=[smem, smem, hbm, hbm, hbm, hbm],
        scratch_shapes=scratch + sems,
        compiler_params=pltpu.CompilerParams(vmem_limit_bytes=51 << 20),
        name="grams",
    )(experts, count, teacher, student, gate, up)


def join_kernel(scaling, own, msg, *rest):
    count, rows, width = own.shape
    panels = width // LANES
    step = read_step(msg)
    if count == 1:
        (out,) = rest
        out[...] = (own[0] + read_block(msg, 0, rows, panels, step)) * scaling
        return
    keep, send, held = rest
    half = count // 2
    for k in range(half):
        held[k] = own[half + k] + read_block(msg, half + k, rows, panels, step)
    write_codes([lambda k=k: held[k] for k in range(half)], send)
    for k in range(half):
        keep[k] = own[k] + read_block(msg, k, rows, panels, step)


def join(own, msg, scaling):
    count, rows, width = own.shape
    if count == 1:
        out_shape = jax.ShapeDtypeStruct((rows, width), jnp.float32)
        scratch = []
    else:
        half = count // 2
        out_shape = (
            jax.ShapeDtypeStruct((half, rows, width), jnp.float32),
            message_shape(half, rows, width),
        )
        scratch = [pltpu.VMEM((half, rows, width), jnp.float32)]
    return pl.pallas_call(
        functools.partial(join_kernel, scaling),
        out_shape=out_shape,
        scratch_shapes=scratch,
        compiler_params=pltpu.CompilerParams(vmem_limit_bytes=32 << 20),
        name=f"join{count}",
    )(own, msg)


def local(teacher, student, experts, count, gate, up):
    ranks = lax.axis_size("dp")
    block = teacher.shape[0] // experts.shape[0]
    scaling = 1.0 / (block * ranks)
    total_rows = gate.shape[0] * gate.shape[2]
    rows = total_rows // ranks
    bits = ranks.bit_length() - 1
    coded = ranks >= 4 and ranks == 1 << bits and rows % 16 == 0 and gate.shape[2] % rows == 0
    if not coded:
        acc = grams(teacher, student, experts, count, gate, up, ranks, None)
        return lax.psum_scatter(acc, "dp", scatter_dimension=0, tiled=True) * scaling
    first = [1 << i for i in range(bits - 1)]
    second = first[1:2] + first[:1] + first[2:]
    own, msg = grams(teacher, student, experts, count, gate, up, ranks, (first, second))
    msg = lax.ppermute(msg, "dp", [(p, p ^ 1) for p in range(ranks)])
    for one, other in zip(first, second):
        own, msg = join(own, msg, scaling)
        msg = lax.ppermute(
            msg, "dp", [(p, p ^ (2 * (other if p % 2 else one))) for p in range(ranks)]
        )
    return join(own, msg, scaling)


def solution(mesh):
    return jax.shard_map(
        local,
        mesh=mesh,
        in_specs=(
            P(("groups", "dp"), None),
            P(("groups", "dp"), None),
            P(("groups", "dp")),
            P(("groups", "dp")),
            P("groups", None, None),
            P("groups", None, None),
        ),
        out_specs=P(("groups", "dp"), None),
        check_vma=False,
    )
```

```python
import functools

import jax
import jax.numpy as jnp
from jax import lax
from jax.experimental import pallas as pl
from jax.experimental.pallas import tpu as pltpu
from jax.sharding import PartitionSpec as P

LANES = 128
TAIL = 16
TOP = 32700.0


def code_scale(exponent, mantissa):
    return (mantissa * (1.0 / 16384.0)) * jnp.exp2(exponent)


def write_codes(blocks, msg_ref):
    rows, width = blocks[0]().shape
    panels = width // LANES
    top = None
    for load in blocks:
        high = jnp.max(jnp.abs(load()), axis=0, keepdims=True)
        for c in range(panels):
            part = high[:, c * LANES : (c + 1) * LANES]
            top = part if top is None else jnp.maximum(top, part)
    exponent = jnp.clip(jnp.ceil(jnp.log2(jnp.maximum(top, 1e-30))), -100.0, 100.0)
    mantissa = jnp.ceil(top * jnp.exp2(-exponent) * 16384.0) + 1.0
    factor = TOP / code_scale(exponent, mantissa)
    for k, load in enumerate(blocks):
        for c in range(panels):
            part = load()[:, c * LANES : (c + 1) * LANES] * factor
            at = (k * panels + c) * rows
            msg_ref[at : at + rows, :] = jnp.round(part).astype(jnp.int32).astype(jnp.int16)
    line = lax.broadcasted_iota(jnp.int32, (TAIL, LANES), 0)
    tail = jnp.where(line == 0, exponent.astype(jnp.int32), mantissa.astype(jnp.int32))
    msg_ref[len(blocks) * panels * rows :, :] = tail.astype(jnp.int16)


def read_step(msg_ref):
    at = msg_ref.shape[0] - TAIL
    tail = msg_ref[at:, :].astype(jnp.int32).astype(jnp.float32)
    return code_scale(tail[0:1], tail[1:2]) * (1.0 / TOP)


def read_block(msg_ref, k, rows, panels, step):
    parts = []
    for c in range(panels):
        at = (k * panels + c) * rows
        parts.append(msg_ref[at : at + rows, :].astype(jnp.int32).astype(jnp.float32) * step)
    return jnp.concatenate(parts, axis=1)


def message_shape(count, rows, width):
    return jax.ShapeDtypeStruct((count * rows * (width // LANES) + TAIL, LANES), jnp.int16)


def block_offsets(groups, core):
    offsets = [0]
    for group in groups:
        offsets = [a ^ b for a in offsets for b in [0, *stage_offsets(group, core)]]
    return offsets


def stage_offsets(group, core):
    if len(group) == 1:
        return list(group)
    one, two = group if core == 0 else group[::-1]
    return [one | two, one, two]


def gram_kernel(
    plan, experts, count, teacher, student, gate, up, *rest
):
    if plan is None:
        acc, x, w, hid, masked, x_sem, w_sem = rest
    else:
        own, msg, x, w, hid, masked, acc, x_sem, w_sem = rest
    slots, both, _ = x.shape
    block = both // 2
    expert_total, _, two = w.shape
    width = two // 2
    live = count[0]

    def fresh(s):
        ok = s < live
        for t in range(s):
            ok = ok & (experts[t] != experts[s])
        return ok

    def x_copies(s):
        rows = pl.ds(s * block, block)
        return [
            pltpu.make_async_copy(student.at[rows], x.at[s, pl.ds(0, block)], x_sem.at[s, 0]),
            pltpu.make_async_copy(teacher.at[rows], x.at[s, pl.ds(block, block)], x_sem.at[s, 1]),
        ]

    def w_copies(e):
        return [
            pltpu.make_async_copy(gate.at[e], w.at[e, :, pl.ds(0, width)], w_sem.at[e, 0]),
            pltpu.make_async_copy(up.at[e], w.at[e, :, pl.ds(width, width)], w_sem.at[e, 1]),
        ]

    for s in range(slots):

        @pl.when(fresh(s))
        def _():
            for copy in w_copies(experts[s]):
                copy.start()

        @pl.when(s < live)
        def _():
            for copy in x_copies(s):
                copy.start()

    for s in range(slots):
        rows = pl.ds(s * block, block)

        @pl.when(fresh(s))
        def _():
            for copy in w_copies(experts[s]):
                copy.wait()

        @pl.when(s < live)
        def _():
            for copy in x_copies(s):
                copy.wait()
            expert = experts[s]
            out = jnp.dot(x[s], w[expert], preferred_element_type=jnp.float32)
            gate_out = out[:, :width]
            hidden = (gate_out / (1.0 + jnp.exp(-gate_out)) * out[:, width:]).astype(jnp.bfloat16)
            hid[rows, :width] = hidden[:block]
            hid[rows, width:] = hidden[block:]
            for e in range(expert_total):
                masked[e, rows] = jnp.where(expert == e, hidden[:block], jnp.zeros_like(hidden[:block]))

        @pl.when(s >= live)
        def _():
            hid[rows] = jnp.zeros((block, two), jnp.bfloat16)
            for e in range(expert_total):
                masked[e, rows] = jnp.zeros((block, width), jnp.bfloat16)

    for e in range(expert_total):
        gram = lax.dot_general(
            masked[e], hid[...], (((0,), (0,)), ((), ())), preferred_element_type=jnp.float32
        )
        if plan is None:
            acc[e * width : (e + 1) * width] = gram
        else:
            rows = acc.shape[1]
            per = width // rows
            acc[e * per : (e + 1) * per] = gram.reshape(per, rows, two)

    if plan is not None:
        me = lax.axis_index("dp")
        core = lax.rem(me, 2)
        chip = me // 2
        tables = [block_offsets(plan, c) for c in (0, 1)]
        loads = []
        for k in range(len(tables[0])):
            mine = jnp.where(core == 0, tables[0][k], tables[1][k])
            theirs = jnp.where(core == 0, tables[1][k], tables[0][k])
            own[k] = acc[2 * (chip ^ mine) + core]
            there = 2 * (chip ^ theirs) + (1 - core)
            loads.append(lambda there=there: acc[there])
        write_codes(loads, msg)


def grams(teacher, student, experts, count, gate, up, ranks, plan):
    slots = experts.shape[0]
    block = teacher.shape[0] // slots
    depth = teacher.shape[1]
    expert_total, _, width = gate.shape
    two = 2 * width
    rows = expert_total * width // ranks
    scratch = [
        pltpu.VMEM((slots, 2 * block, depth), jnp.bfloat16),
        pltpu.VMEM((expert_total, depth, two), jnp.bfloat16),
        pltpu.VMEM((slots * block, two), jnp.bfloat16),
        pltpu.VMEM((expert_total, slots * block, width), jnp.bfloat16),
    ]
    sems = [pltpu.SemaphoreType.DMA((slots, 2)), pltpu.SemaphoreType.DMA((expert_total, 2))]
    if plan is None:
        out_shape = jax.ShapeDtypeStruct((expert_total * width, two), jnp.float32)
    else:
        scratch.append(pltpu.VMEM((ranks, rows, two), jnp.float32))
        out_shape = (
            jax.ShapeDtypeStruct((ranks // 2, rows, two), jnp.float32),
            message_shape(ranks // 2, rows, two),
        )
    smem = pl.BlockSpec(memory_space=pltpu.SMEM)
    hbm = pl.BlockSpec(memory_space=pl.ANY)
    return pl.pallas_call(
        functools.partial(gram_kernel, plan),
        out_shape=out_shape,
        in_specs=[smem, smem, hbm, hbm, hbm, hbm],
        scratch_shapes=scratch + sems,
        compiler_params=pltpu.CompilerParams(vmem_limit_bytes=51 << 20),
        name="grams",
    )(experts, count, teacher, student, gate, up)


def join_kernel(scaling, radix, parts, own, *rest):
    count, rows, width = own.shape
    panels = width // LANES
    msgs = rest[:parts]
    steps = [read_step(msg) for msg in msgs]

    def total(k):
        return own[k] + sum(
            read_block(msg, k, rows, panels, step) for msg, step in zip(msgs, steps)
        )

    if radix == 1:
        rest[parts][...] = total(0) * scaling
        return
    keep, *sends, held = rest[parts:]
    per = count // radix
    for k in range(per, count):
        held[k - per] = total(k)
    for d, send in enumerate(sends):
        write_codes([lambda k=k: held[k] for k in range(d * per, (d + 1) * per)], send)
    for k in range(per):
        keep[k] = total(k)


def join(own, msgs, radix, scaling):
    count, rows, width = own.shape
    if radix == 1:
        out_shape = jax.ShapeDtypeStruct((rows, width), jnp.float32)
        scratch = []
    else:
        per = count // radix
        out_shape = (
            jax.ShapeDtypeStruct((per, rows, width), jnp.float32),
            *[message_shape(per, rows, width)] * (radix - 1),
        )
        scratch = [pltpu.VMEM((count - per, rows, width), jnp.float32)]
    return pl.pallas_call(
        functools.partial(join_kernel, scaling, radix, len(msgs)),
        out_shape=out_shape,
        scratch_shapes=scratch,
        compiler_params=pltpu.CompilerParams(vmem_limit_bytes=32 << 20),
        name=f"join{count}",
    )(own, *msgs)


def local(teacher, student, experts, count, gate, up):
    ranks = lax.axis_size("dp")
    block = teacher.shape[0] // experts.shape[0]
    scaling = 1.0 / (block * ranks)
    total_rows = gate.shape[0] * gate.shape[2]
    rows = total_rows // ranks
    bits = ranks.bit_length() - 1
    coded = ranks >= 4 and ranks == 1 << bits and rows % 16 == 0 and gate.shape[2] % rows == 0
    if not coded:
        acc = grams(teacher, student, experts, count, gate, up, ranks, None)
        return lax.psum_scatter(acc, "dp", scatter_dimension=0, tiled=True) * scaling
    chip_bits = [1 << i for i in range(bits - 1)]
    groups = [tuple(chip_bits[i : i + 2]) for i in range(0, len(chip_bits), 2)]
    own, msg = grams(teacher, student, experts, count, gate, up, ranks, groups)
    msgs = [lax.ppermute(msg, "dp", [(p, p ^ 1) for p in range(ranks)])]
    for group in groups:
        own, *msgs = join(own, msgs, 1 << len(group), scaling)
        reach = [stage_offsets(group, core) for core in (0, 1)]
        msgs = [
            lax.ppermute(msg, "dp", [(p, p ^ (2 * reach[p % 2][i])) for p in range(ranks)])
            for i, msg in enumerate(msgs)
        ]
    return join(own, msgs, 1, scaling)


def solution(mesh):
    return jax.shard_map(
        local,
        mesh=mesh,
        in_specs=(
            P(("groups", "dp"), None),
            P(("groups", "dp"), None),
            P(("groups", "dp")),
            P(("groups", "dp")),
            P("groups", None, None),
            P("groups", None, None),
        ),
        out_specs=P(("groups", "dp"), None),
        check_vma=False,
    )
```

```python
import functools

import jax
import jax.numpy as jnp
from jax import lax
from jax.experimental import pallas as pl
from jax.experimental.pallas import tpu as pltpu
from jax.sharding import PartitionSpec as P

LANES = 128
TAIL = 16
TOP = 32700.0
LEAST = 2.0**-110


def code_scale(exponent, mantissa):
    return (mantissa * (1.0 / 16384.0)) * jnp.exp2(exponent)


def write_codes(blocks, msg_ref):
    rows, width = blocks[0]().shape
    panels = width // LANES
    top = None
    for load in blocks:
        high = jnp.max(jnp.abs(load()), axis=0, keepdims=True)
        for c in range(panels):
            part = high[:, c * LANES : (c + 1) * LANES]
            top = part if top is None else jnp.maximum(top, part)
    top = jnp.maximum(top, LEAST)
    exponent = jnp.ceil(jnp.log2(top))
    mantissa = jnp.ceil(top * jnp.exp2(-exponent) * 16384.0) + 1.0
    factor = TOP / code_scale(exponent, mantissa)
    for k, load in enumerate(blocks):
        for c in range(panels):
            part = load()[:, c * LANES : (c + 1) * LANES] * factor
            at = (k * panels + c) * rows
            msg_ref[at : at + rows, :] = jnp.round(part).astype(jnp.int32).astype(jnp.int16)
    line = lax.broadcasted_iota(jnp.int32, (TAIL, LANES), 0)
    tail = jnp.where(line == 0, exponent.astype(jnp.int32), mantissa.astype(jnp.int32))
    msg_ref[len(blocks) * panels * rows :, :] = tail.astype(jnp.int16)


def read_step(msg_ref):
    at = msg_ref.shape[0] - TAIL
    tail = msg_ref[at:, :].astype(jnp.int32).astype(jnp.float32)
    return code_scale(tail[0:1], tail[1:2]) * (1.0 / TOP)


def read_block(msg_ref, k, rows, panels, step):
    parts = []
    for c in range(panels):
        at = (k * panels + c) * rows
        parts.append(msg_ref[at : at + rows, :].astype(jnp.int32).astype(jnp.float32) * step)
    return jnp.concatenate(parts, axis=1)


def message_shape(count, rows, width):
    return jax.ShapeDtypeStruct((count * rows * (width // LANES) + TAIL, LANES), jnp.int16)


def block_offsets(groups, core):
    offsets = [0]
    for group in groups:
        offsets = [a ^ b for a in offsets for b in [0, *stage_offsets(group, core)]]
    return offsets


def stage_offsets(group, core):
    if len(group) == 1:
        return list(group)
    one, two = group if core == 0 else group[::-1]
    return [one | two, one, two]


def gram_kernel(plan, experts_in, count, teacher, student, gate, up, *rest):
    if plan is None:
        acc, x, w, hid, order, experts, x_sem, w_sem, s_sem = rest
    else:
        own, msg, x, w, hid, order, experts, acc, x_sem, w_sem, s_sem = rest
    slots, both, _ = x.shape
    block = both // 2
    expert_total, panels, _, pair_width = w.shape
    lanes = pair_width // 2
    width = panels * lanes

    def w_copies(e, c):
        cols = pl.ds(c * lanes, lanes)
        return [
            pltpu.make_async_copy(gate.at[e, :, cols], w.at[e, c, :, pl.ds(0, lanes)], w_sem.at[e, c, 0]),
            pltpu.make_async_copy(up.at[e, :, cols], w.at[e, c, :, pl.ds(lanes, lanes)], w_sem.at[e, c, 1]),
        ]

    scalars = [
        pltpu.make_async_copy(experts_in, experts, s_sem.at[0]),
    ]
    for copy in scalars:
        copy.start()
    for c in range(panels):
        for copy in w_copies(0, c):
            copy.start()
    for copy in scalars:
        copy.wait()
    live = count[0]

    keys = [jnp.where(s < live, experts[s], experts[s] + expert_total) for s in range(slots)]
    for s in range(slots):
        place = jnp.int32(0)
        for t in range(slots):
            if t != s:
                ahead = keys[t] <= keys[s] if t < s else keys[t] < keys[s]
                place = place + ahead.astype(jnp.int32)
        order[place] = s

    def expert_at(i):
        return experts[order[i]]

    def fresh(i):
        new = expert_at(i) != (expert_at(i - 1) if i else 0)
        return (i < live) & new

    def x_copies(i):
        rows = pl.ds(order[i] * block, block)
        return [
            pltpu.make_async_copy(student.at[rows], x.at[i, pl.ds(0, block)], x_sem.at[i, 0]),
            pltpu.make_async_copy(teacher.at[rows], x.at[i, pl.ds(block, block)], x_sem.at[i, 1]),
        ]

    def start_w(i):
        @pl.when(fresh(i))
        def _():
            for c in range(panels):
                for copy in w_copies(expert_at(i), c):
                    copy.start()

    def start_x(i):
        @pl.when(i < live)
        def _():
            for copy in x_copies(i):
                copy.start()

    def wait_w(i):
        @pl.when(fresh(i))
        def _():
            for c in range(panels):
                for copy in w_copies(expert_at(i), c):
                    copy.wait()

    def wait_x(i):
        @pl.when(i < live)
        def _():
            for copy in x_copies(i):
                copy.wait()

    start_x(0)
    start_w(0)
    acc[...] = jnp.zeros_like(acc)

    def hide(i):
        expert = expert_at(i)
        rows = pl.ds(i * block, block)
        for c in range(panels):
            out = jnp.dot(x[i], w[expert, c], preferred_element_type=jnp.float32)
            gate_out = out[:, :lanes]
            part = (gate_out / (1.0 + jnp.exp(-gate_out)) * out[:, lanes:]).astype(jnp.bfloat16)
            hid[rows, c * lanes : (c + 1) * lanes] = part[:block]
            hid[rows, width + c * lanes : width + (c + 1) * lanes] = part[block:]

    def add_product(expert, left, right):
        gram = lax.dot_general(left, right, (((0,), (0,)), ((), ())), preferred_element_type=jnp.float32)
        if plan is None:
            at = pl.ds(expert * width, width)
            acc[at] = acc[at] + gram
        else:
            per = width // acc.shape[1]
            at = pl.ds(expert * per, per)
            acc[at] = acc[at] + gram.reshape(per, *acc.shape[1:])

    def add_gram(i):
        rows = pl.ds(pl.multiple_of(i * block, block), block)
        add_product(expert_at(i), hid[rows, :width], hid[rows])

    for copy in w_copies(0, 0):
        copy.wait()
    for i in range(1, slots):
        start_w(i)
        start_x(i)
    wait_x(0)
    for c in range(1, panels):
        for copy in w_copies(0, c):
            copy.wait()
    wait_w(0)
    hide(0)

    @pl.when(live == slots)
    def _():
        for first, end in [(1, min(2, slots)), (2, slots)]:
            for i in range(first, end):
                wait_w(i)
            for i in range(first, end):
                for copy in x_copies(i):
                    copy.wait()
            for i in range(first, end):
                hide(i)
        for i in range(0, slots - 1, 2):
            same = expert_at(i) == expert_at(i + 1)
            two_rows = pl.ds(i * block, 2 * block)
            one_row = pl.ds((i + 1) * block, block)
            other = hid[one_row, :width]
            left = jnp.concatenate(
                [hid[pl.ds(i * block, block), :width], jnp.where(same, other, jnp.zeros_like(other))]
            )
            add_product(expert_at(i), left, hid[two_rows])
        for i in range(0, slots - 1, 2):

            @pl.when(expert_at(i) != expert_at(i + 1))
            def _():
                add_gram(i + 1)

        if slots % 2:
            add_gram(slots - 1)

    @pl.when(live < slots)
    def _():
        for i in range(1, slots - 1):

            @pl.when(i < live)
            def _():
                wait_w(i)
                for copy in x_copies(i):
                    copy.wait()
                hide(i)
                add_gram(i - 1)

        add_gram(live - 1)

    if plan is not None:
        me = lax.axis_index("dp")
        core = lax.rem(me, 2)
        chip = me // 2
        tables = [block_offsets(plan, c) for c in (0, 1)]
        loads = []
        for k in range(len(tables[0])):
            mine = jnp.where(core == 0, tables[0][k], tables[1][k])
            theirs = jnp.where(core == 0, tables[1][k], tables[0][k])
            own[k] = acc[2 * (chip ^ mine) + core]
            there = 2 * (chip ^ theirs) + (1 - core)
            loads.append(lambda there=there: acc[there])
        write_codes(loads, msg)


def grams(teacher, student, experts, count, gate, up, ranks, plan):
    slots = experts.shape[0]
    block = teacher.shape[0] // slots
    depth = teacher.shape[1]
    expert_total, _, width = gate.shape
    two = 2 * width
    rows = expert_total * width // ranks
    panels = width // LANES
    scratch = [
        pltpu.VMEM((slots, 2 * block, depth), jnp.bfloat16),
        pltpu.VMEM((expert_total, panels, depth, 2 * LANES), jnp.bfloat16),
        pltpu.VMEM((slots * block, two), jnp.bfloat16),
        pltpu.SMEM((slots,), jnp.int32),
        pltpu.SMEM((slots,), jnp.int32),
    ]
    sems = [
        pltpu.SemaphoreType.DMA((slots, 2)),
        pltpu.SemaphoreType.DMA((expert_total, panels, 2)),
        pltpu.SemaphoreType.DMA((1,)),
    ]
    if plan is None:
        out_shape = jax.ShapeDtypeStruct((expert_total * width, two), jnp.float32)
    else:
        scratch.append(pltpu.VMEM((ranks, rows, two), jnp.float32))
        out_shape = (
            jax.ShapeDtypeStruct((ranks // 2, rows, two), jnp.float32),
            message_shape(ranks // 2, rows, two),
        )
    hbm = pl.BlockSpec(memory_space=pl.ANY)
    return pl.pallas_call(
        functools.partial(gram_kernel, plan),
        out_shape=out_shape,
        in_specs=[hbm, pl.BlockSpec(memory_space=pltpu.SMEM), hbm, hbm, hbm, hbm],
        scratch_shapes=scratch + sems,
        compiler_params=pltpu.CompilerParams(vmem_limit_bytes=51 << 20),
        name="grams",
    )(pltpu.with_memory_space_constraint(experts, pltpu.HBM), count, *[pltpu.with_memory_space_constraint(a, pltpu.HBM) for a in (teacher, student, gate, up)])


def join_kernel(scaling, radix, parts, own, *rest):
    count, rows, width = own.shape
    panels = width // LANES
    msgs = rest[:parts]
    steps = [read_step(msg) for msg in msgs]

    def total(k):
        return own[k] + sum(
            read_block(msg, k, rows, panels, step) for msg, step in zip(msgs, steps)
        )

    if radix == 1:
        rest[parts][...] = total(0) * scaling
        return
    keep, *sends, held = rest[parts:]
    per = count // radix
    for k in range(per, count):
        held[k - per] = total(k)
    for d, send in enumerate(sends):
        write_codes([lambda k=k: held[k] for k in range(d * per, (d + 1) * per)], send)
    for k in range(per):
        keep[k] = total(k)


def join(own, msgs, radix, scaling):
    count, rows, width = own.shape
    if radix == 1:
        out_shape = jax.ShapeDtypeStruct((rows, width), jnp.float32)
        scratch = []
    else:
        per = count // radix
        out_shape = (
            jax.ShapeDtypeStruct((per, rows, width), jnp.float32),
            *[message_shape(per, rows, width)] * (radix - 1),
        )
        scratch = [pltpu.VMEM((count - per, rows, width), jnp.float32)]
    return pl.pallas_call(
        functools.partial(join_kernel, scaling, radix, len(msgs)),
        out_shape=out_shape,
        scratch_shapes=scratch,
        compiler_params=pltpu.CompilerParams(vmem_limit_bytes=32 << 20),
        name=f"join{count}",
    )(own, *msgs)


def local(teacher, student, experts, count, gate, up):
    ranks = lax.axis_size("dp")
    block = teacher.shape[0] // experts.shape[0]
    scaling = 1.0 / (block * ranks)
    total_rows = gate.shape[0] * gate.shape[2]
    rows = total_rows // ranks
    bits = ranks.bit_length() - 1
    coded = ranks >= 4 and ranks == 1 << bits and rows % 16 == 0 and gate.shape[2] % rows == 0
    if not coded:
        acc = grams(teacher, student, experts, count, gate, up, ranks, None)
        return lax.psum_scatter(acc, "dp", scatter_dimension=0, tiled=True) * scaling
    chip_bits = [1 << i for i in range(bits - 1)]
    groups = [tuple(chip_bits[i : i + 2]) for i in range(0, len(chip_bits), 2)]
    own, msg = grams(teacher, student, experts, count, gate, up, ranks, groups)
    msgs = [lax.ppermute(msg, "dp", [(p, p ^ 1) for p in range(ranks)])]
    for group in groups:
        own, *msgs = join(own, msgs, 1 << len(group), scaling)
        reach = [stage_offsets(group, core) for core in (0, 1)]
        msgs = [
            lax.ppermute(msg, "dp", [(p, p ^ (2 * reach[p % 2][i])) for p in range(ranks)])
            for i, msg in enumerate(msgs)
        ]
    return join(own, msgs, 1, scaling)


def solution(mesh):
    return jax.shard_map(
        local,
        mesh=mesh,
        in_specs=(
            P(("groups", "dp"), None),
            P(("groups", "dp"), None),
            P(("groups", "dp")),
            P(("groups", "dp")),
            P("groups", None, None),
            P("groups", None, None),
        ),
        out_specs=P(("groups", "dp"), None),
        check_vma=False,
    )
```

```python
import functools

import jax
import jax.numpy as jnp
from jax import lax
from jax.experimental import pallas as pl
from jax.experimental.pallas import tpu as pltpu
from jax.sharding import PartitionSpec as P

LANES = 128
TAIL = 16
TOP = 32700.0
LEAST = 2.0**-110


def code_scale(exponent, mantissa):
    return (mantissa * (1.0 / 16384.0)) * jnp.exp2(exponent)


def write_codes(blocks, msg_ref):
    rows, width = blocks[0]().shape
    panels = width // LANES
    top = None
    for load in blocks:
        high = jnp.max(jnp.abs(load()), axis=0, keepdims=True)
        for c in range(panels):
            part = high[:, c * LANES : (c + 1) * LANES]
            top = part if top is None else jnp.maximum(top, part)
    top = jnp.maximum(top, LEAST)
    exponent = jnp.ceil(jnp.log2(top))
    mantissa = jnp.ceil(top * jnp.exp2(-exponent) * 16384.0) + 1.0
    factor = TOP / code_scale(exponent, mantissa)
    for k, load in enumerate(blocks):
        for c in range(panels):
            part = load()[:, c * LANES : (c + 1) * LANES] * factor
            at = (k * panels + c) * rows
            msg_ref[at : at + rows, :] = jnp.round(part).astype(jnp.int32).astype(jnp.int16)
    line = lax.broadcasted_iota(jnp.int32, (TAIL, LANES), 0)
    tail = jnp.where(line == 0, exponent.astype(jnp.int32), mantissa.astype(jnp.int32))
    msg_ref[len(blocks) * panels * rows :, :] = tail.astype(jnp.int16)


def read_step(msg_ref):
    at = msg_ref.shape[0] - TAIL
    tail = msg_ref[at:, :].astype(jnp.int32).astype(jnp.float32)
    return code_scale(tail[0:1], tail[1:2]) * (1.0 / TOP)


def read_block(msg_ref, k, rows, panels, step):
    parts = []
    for c in range(panels):
        at = (k * panels + c) * rows
        parts.append(msg_ref[at : at + rows, :].astype(jnp.int32).astype(jnp.float32) * step)
    return jnp.concatenate(parts, axis=1)


def message_shape(count, rows, width):
    return jax.ShapeDtypeStruct((count * rows * (width // LANES) + TAIL, LANES), jnp.int16)


def block_offsets(plan, core):
    offsets = [0]
    for group in plan[core]:
        offsets = [a ^ b for a in offsets for b in [0, *stage_offsets(group, core)]]
    return offsets


def stage_offsets(group, core):
    if len(group) == 1:
        return list(group)
    one, two = group if core == 0 else group[::-1]
    return [one | two, one, two]


def gram_kernel(plan, experts_in, count, teacher, student, gate, up, *rest):
    if plan is None:
        acc, x, w, hid, order, experts, x_sem, w_sem, s_sem = rest
    else:
        own, msg, x, w, hid, order, experts, acc, x_sem, w_sem, s_sem = rest
    slots, both, _ = x.shape
    block = both // 2
    expert_total, panels, _, pair_width = w.shape
    lanes = pair_width // 2
    width = panels * lanes

    def w_copies(e, c):
        cols = pl.ds(c * lanes, lanes)
        return [
            pltpu.make_async_copy(gate.at[e, :, cols], w.at[e, c, :, pl.ds(0, lanes)], w_sem.at[e, c, 0]),
            pltpu.make_async_copy(up.at[e, :, cols], w.at[e, c, :, pl.ds(lanes, lanes)], w_sem.at[e, c, 1]),
        ]

    scalars = [
        pltpu.make_async_copy(experts_in, experts, s_sem.at[0]),
    ]
    for copy in scalars:
        copy.start()
    for c in range(panels):
        for copy in w_copies(0, c):
            copy.start()
    for copy in scalars:
        copy.wait()
    live = count[0]

    keys = [jnp.where(s < live, experts[s], experts[s] + expert_total) for s in range(slots)]
    for s in range(slots):
        place = jnp.int32(0)
        for t in range(slots):
            if t != s:
                ahead = keys[t] <= keys[s] if t < s else keys[t] < keys[s]
                place = place + ahead.astype(jnp.int32)
        order[place] = s

    def expert_at(i):
        return experts[order[i]]

    def fresh(i):
        new = expert_at(i) != (expert_at(i - 1) if i else 0)
        return (i < live) & new

    def x_copies(i):
        rows = pl.ds(order[i] * block, block)
        return [
            pltpu.make_async_copy(student.at[rows], x.at[i, pl.ds(0, block)], x_sem.at[i, 0]),
            pltpu.make_async_copy(teacher.at[rows], x.at[i, pl.ds(block, block)], x_sem.at[i, 1]),
        ]

    def start_w(i):
        @pl.when(fresh(i))
        def _():
            for c in range(panels):
                for copy in w_copies(expert_at(i), c):
                    copy.start()

    def start_x(i):
        @pl.when(i < live)
        def _():
            for copy in x_copies(i):
                copy.start()

    def wait_w(i):
        @pl.when(fresh(i))
        def _():
            for c in range(panels):
                for copy in w_copies(expert_at(i), c):
                    copy.wait()

    def wait_x(i):
        @pl.when(i < live)
        def _():
            for copy in x_copies(i):
                copy.wait()

    start_x(0)
    start_w(0)
    acc[...] = jnp.zeros_like(acc)

    def hide(i):
        expert = expert_at(i)
        rows = pl.ds(i * block, block)
        for c in range(panels):
            out = jnp.dot(x[i], w[expert, c], preferred_element_type=jnp.float32)
            gate_out = out[:, :lanes]
            part = (gate_out / (1.0 + jnp.exp(-gate_out)) * out[:, lanes:]).astype(jnp.bfloat16)
            hid[rows, c * lanes : (c + 1) * lanes] = part[:block]
            hid[rows, width + c * lanes : width + (c + 1) * lanes] = part[block:]

    def add_product(expert, left, right):
        gram = lax.dot_general(left, right, (((0,), (0,)), ((), ())), preferred_element_type=jnp.float32)
        if plan is None:
            at = pl.ds(expert * width, width)
            acc[at] = acc[at] + gram
        else:
            per = width // acc.shape[1]
            at = pl.ds(expert * per, per)
            acc[at] = acc[at] + gram.reshape(per, *acc.shape[1:])

    def add_gram(i):
        rows = pl.ds(pl.multiple_of(i * block, block), block)
        add_product(expert_at(i), hid[rows, :width], hid[rows])

    for copy in w_copies(0, 0):
        copy.wait()
    for i in range(1, slots):
        start_w(i)
        start_x(i)
    wait_x(0)
    for c in range(1, panels):
        for copy in w_copies(0, c):
            copy.wait()
    wait_w(0)
    hide(0)

    @pl.when(live == slots)
    def _():
        for first, end in [(1, min(2, slots)), (2, slots)]:
            for i in range(first, end):
                wait_w(i)
            for i in range(first, end):
                for copy in x_copies(i):
                    copy.wait()
            for i in range(first, end):
                hide(i)
        for i in range(0, slots - 1, 2):
            same = expert_at(i) == expert_at(i + 1)
            two_rows = pl.ds(i * block, 2 * block)
            one_row = pl.ds((i + 1) * block, block)
            other = hid[one_row, :width]
            left = jnp.concatenate(
                [hid[pl.ds(i * block, block), :width], jnp.where(same, other, jnp.zeros_like(other))]
            )
            add_product(expert_at(i), left, hid[two_rows])
        for i in range(0, slots - 1, 2):

            @pl.when(expert_at(i) != expert_at(i + 1))
            def _():
                add_gram(i + 1)

        if slots % 2:
            add_gram(slots - 1)

    @pl.when(live < slots)
    def _():
        for i in range(1, slots - 1):

            @pl.when(i < live)
            def _():
                wait_w(i)
                for copy in x_copies(i):
                    copy.wait()
                hide(i)
                add_gram(i - 1)

        add_gram(live - 1)

    if plan is not None:
        me = lax.axis_index("dp")
        core = lax.rem(me, 2)
        chip = me // 2
        tables = [block_offsets(plan, c) for c in (0, 1)]
        loads = []
        for k in range(len(tables[0])):
            mine = jnp.where(core == 0, tables[0][k], tables[1][k])
            theirs = jnp.where(core == 0, tables[1][k], tables[0][k])
            own[k] = acc[2 * (chip ^ mine) + core]
            there = 2 * (chip ^ theirs) + (1 - core)
            loads.append(lambda there=there: acc[there])
        write_codes(loads, msg)


def grams(teacher, student, experts, count, gate, up, ranks, plan):
    slots = experts.shape[0]
    block = teacher.shape[0] // slots
    depth = teacher.shape[1]
    expert_total, _, width = gate.shape
    two = 2 * width
    rows = expert_total * width // ranks
    panels = width // LANES
    scratch = [
        pltpu.VMEM((slots, 2 * block, depth), jnp.bfloat16),
        pltpu.VMEM((expert_total, panels, depth, 2 * LANES), jnp.bfloat16),
        pltpu.VMEM((slots * block, two), jnp.bfloat16),
        pltpu.SMEM((slots,), jnp.int32),
        pltpu.SMEM((slots,), jnp.int32),
    ]
    sems = [
        pltpu.SemaphoreType.DMA((slots, 2)),
        pltpu.SemaphoreType.DMA((expert_total, panels, 2)),
        pltpu.SemaphoreType.DMA((1,)),
    ]
    if plan is None:
        out_shape = jax.ShapeDtypeStruct((expert_total * width, two), jnp.float32)
    else:
        scratch.append(pltpu.VMEM((ranks, rows, two), jnp.float32))
        out_shape = (
            jax.ShapeDtypeStruct((ranks // 2, rows, two), jnp.float32),
            message_shape(ranks // 2, rows, two),
        )
    hbm = pl.BlockSpec(memory_space=pl.ANY)
    return pl.pallas_call(
        functools.partial(gram_kernel, plan),
        out_shape=out_shape,
        in_specs=[hbm, pl.BlockSpec(memory_space=pltpu.SMEM), hbm, hbm, hbm, hbm],
        scratch_shapes=scratch + sems,
        compiler_params=pltpu.CompilerParams(vmem_limit_bytes=51 << 20),
        name="grams",
    )(pltpu.with_memory_space_constraint(experts, pltpu.HBM), count, *[pltpu.with_memory_space_constraint(a, pltpu.HBM) for a in (teacher, student, gate, up)])


def join_kernel(scaling, radix, parts, own, *rest):
    count, rows, width = own.shape
    panels = width // LANES
    msgs = rest[:parts]
    steps = [read_step(msg) for msg in msgs]

    def total(k):
        return own[k] + sum(
            read_block(msg, k, rows, panels, step) for msg, step in zip(msgs, steps)
        )

    if radix == 1:
        rest[parts][...] = total(0) * scaling
        return
    keep, *sends, held = rest[parts:]
    per = count // radix
    for k in range(per, count):
        held[k - per] = total(k)
    for d, send in enumerate(sends):
        write_codes([lambda k=k: held[k] for k in range(d * per, (d + 1) * per)], send)
    for k in range(per):
        keep[k] = total(k)


def join(own, msgs, radix, scaling):
    count, rows, width = own.shape
    if radix == 1:
        out_shape = jax.ShapeDtypeStruct((rows, width), jnp.float32)
        scratch = []
    else:
        per = count // radix
        out_shape = (
            jax.ShapeDtypeStruct((per, rows, width), jnp.float32),
            *[message_shape(per, rows, width)] * (radix - 1),
        )
        scratch = [pltpu.VMEM((count - per, rows, width), jnp.float32)]
    return pl.pallas_call(
        functools.partial(join_kernel, scaling, radix, len(msgs)),
        out_shape=out_shape,
        scratch_shapes=scratch,
        compiler_params=pltpu.CompilerParams(vmem_limit_bytes=32 << 20),
        name=f"join{count}",
    )(own, *msgs)


def local(teacher, student, experts, count, gate, up):
    ranks = lax.axis_size("dp")
    block = teacher.shape[0] // experts.shape[0]
    scaling = 1.0 / (block * ranks)
    total_rows = gate.shape[0] * gate.shape[2]
    rows = total_rows // ranks
    bits = ranks.bit_length() - 1
    coded = ranks >= 4 and ranks == 1 << bits and rows % 16 == 0 and gate.shape[2] % rows == 0
    if not coded:
        acc = grams(teacher, student, experts, count, gate, up, ranks, None)
        return lax.psum_scatter(acc, "dp", scatter_dimension=0, tiled=True) * scaling
    chip_bits = [1 << i for i in range(bits - 1)]
    orders = [chip_bits, chip_bits[:1] + chip_bits[2:3] + chip_bits[1:2] + chip_bits[3:]]
    plan = [[tuple(bits[i : i + 2]) for i in range(0, len(bits), 2)] for bits in orders]
    own, msg = grams(teacher, student, experts, count, gate, up, ranks, plan)
    msgs = [lax.ppermute(msg, "dp", [(p, p ^ 1) for p in range(ranks)])]
    for pair in zip(*plan):
        own, *msgs = join(own, msgs, 1 << len(pair[0]), scaling)
        reach = [stage_offsets(group, core) for core, group in enumerate(pair)]
        msgs = [
            lax.ppermute(msg, "dp", [(p, p ^ (2 * reach[p % 2][i])) for p in range(ranks)])
            for i, msg in enumerate(msgs)
        ]
    return join(own, msgs, 1, scaling)


def solution(mesh):
    return jax.shard_map(
        local,
        mesh=mesh,
        in_specs=(
            P(("groups", "dp"), None),
            P(("groups", "dp"), None),
            P(("groups", "dp")),
            P(("groups", "dp")),
            P("groups", None, None),
            P("groups", None, None),
        ),
        out_specs=P(("groups", "dp"), None),
        check_vma=False,
    )
```

```python
import functools

import jax
import jax.numpy as jnp
from jax import lax
from jax.experimental import pallas as pl
from jax.experimental.pallas import tpu as pltpu
from jax.sharding import PartitionSpec as P

LANES = 128
TAIL = 16
TOP = 32700.0
LEAST = 2.0**-110


def code_scale(exponent, mantissa):
    return (mantissa * (1.0 / 16384.0)) * jnp.exp2(exponent)


def write_codes(blocks, msg_ref):
    rows, width = blocks[0]().shape
    panels = width // LANES
    top = None
    for load in blocks:
        high = jnp.max(jnp.abs(load()), axis=0, keepdims=True)
        for c in range(panels):
            part = high[:, c * LANES : (c + 1) * LANES]
            top = part if top is None else jnp.maximum(top, part)
    top = jnp.maximum(top, LEAST)
    exponent = jnp.ceil(jnp.log2(top))
    mantissa = jnp.ceil(top * jnp.exp2(-exponent) * 16384.0) + 1.0
    factor = TOP / code_scale(exponent, mantissa)
    for k, load in enumerate(blocks):
        for c in range(panels):
            part = load()[:, c * LANES : (c + 1) * LANES] * factor
            at = (k * panels + c) * rows
            msg_ref[at : at + rows, :] = jnp.round(part).astype(jnp.int32).astype(jnp.int16)
    line = lax.broadcasted_iota(jnp.int32, (TAIL, LANES), 0)
    tail = jnp.where(line == 0, exponent.astype(jnp.int32), mantissa.astype(jnp.int32))
    msg_ref[len(blocks) * panels * rows :, :] = tail.astype(jnp.int16)


def read_step(msg_ref):
    at = msg_ref.shape[0] - TAIL
    tail = msg_ref[at:, :].astype(jnp.int32).astype(jnp.float32)
    return code_scale(tail[0:1], tail[1:2]) * (1.0 / TOP)


def read_block(msg_ref, k, rows, panels, step):
    parts = []
    for c in range(panels):
        at = (k * panels + c) * rows
        parts.append(msg_ref[at : at + rows, :].astype(jnp.int32).astype(jnp.float32) * step)
    return jnp.concatenate(parts, axis=1)


def message_shape(count, rows, width):
    return jax.ShapeDtypeStruct((count * rows * (width // LANES) + TAIL, LANES), jnp.int16)


def block_offsets(plan, core):
    offsets = [0]
    for group in plan[core]:
        offsets = [a ^ b for a in offsets for b in [0, *stage_offsets(group, core)]]
    return offsets


def stage_offsets(group, core):
    if len(group) == 1:
        return list(group)
    one, two = group
    return [one, one | two, two] if core == 0 else [two, one, one | two]


def gram_kernel(plan, experts_in, count, teacher, student, gate, up, *rest):
    if plan is None:
        acc, x, w, hid, order, experts, x_sem, w_sem, s_sem = rest
    else:
        own, msg, x, w, hid, order, experts, acc, x_sem, w_sem, s_sem = rest
    slots, both, _ = x.shape
    block = both // 2
    expert_total, panels, _, pair_width = w.shape
    lanes = pair_width // 2
    width = panels * lanes

    def w_copies(e, c):
        cols = pl.ds(c * lanes, lanes)
        return [
            pltpu.make_async_copy(gate.at[e, :, cols], w.at[e, c, :, pl.ds(0, lanes)], w_sem.at[e, c, 0]),
            pltpu.make_async_copy(up.at[e, :, cols], w.at[e, c, :, pl.ds(lanes, lanes)], w_sem.at[e, c, 1]),
        ]

    scalars = [
        pltpu.make_async_copy(experts_in, experts, s_sem.at[0]),
    ]
    for copy in scalars:
        copy.start()
    for c in range(panels):
        for copy in w_copies(0, c):
            copy.start()
    for copy in scalars:
        copy.wait()
    live = count[0]

    keys = [jnp.where(s < live, experts[s], experts[s] + expert_total) for s in range(slots)]
    for s in range(slots):
        place = jnp.int32(0)
        for t in range(slots):
            if t != s:
                ahead = keys[t] <= keys[s] if t < s else keys[t] < keys[s]
                place = place + ahead.astype(jnp.int32)
        order[place] = s

    def expert_at(i):
        return experts[order[i]]

    def fresh(i):
        new = expert_at(i) != (expert_at(i - 1) if i else 0)
        return (i < live) & new

    def x_copies(i):
        rows = pl.ds(order[i] * block, block)
        return [
            pltpu.make_async_copy(student.at[rows], x.at[i, pl.ds(0, block)], x_sem.at[i, 0]),
            pltpu.make_async_copy(teacher.at[rows], x.at[i, pl.ds(block, block)], x_sem.at[i, 1]),
        ]

    def start_w(i):
        @pl.when(fresh(i))
        def _():
            for c in range(panels):
                for copy in w_copies(expert_at(i), c):
                    copy.start()

    def start_x(i):
        @pl.when(i < live)
        def _():
            for copy in x_copies(i):
                copy.start()

    def wait_w(i):
        @pl.when(fresh(i))
        def _():
            for c in range(panels):
                for copy in w_copies(expert_at(i), c):
                    copy.wait()

    def wait_x(i):
        @pl.when(i < live)
        def _():
            for copy in x_copies(i):
                copy.wait()

    start_x(0)
    start_w(0)
    acc[...] = jnp.zeros_like(acc)

    def hide(i):
        expert = expert_at(i)
        rows = pl.ds(i * block, block)
        for c in range(panels):
            out = jnp.dot(x[i], w[expert, c], preferred_element_type=jnp.float32)
            gate_out = out[:, :lanes]
            part = (gate_out / (1.0 + jnp.exp(-gate_out)) * out[:, lanes:]).astype(jnp.bfloat16)
            hid[rows, c * lanes : (c + 1) * lanes] = part[:block]
            hid[rows, width + c * lanes : width + (c + 1) * lanes] = part[block:]

    def add_product(expert, left, right):
        gram = lax.dot_general(left, right, (((0,), (0,)), ((), ())), preferred_element_type=jnp.float32)
        if plan is None:
            at = pl.ds(expert * width, width)
            acc[at] = acc[at] + gram
        else:
            per = width // acc.shape[1]
            at = pl.ds(expert * per, per)
            acc[at] = acc[at] + gram.reshape(per, *acc.shape[1:])

    def add_gram(i):
        rows = pl.ds(pl.multiple_of(i * block, block), block)
        add_product(expert_at(i), hid[rows, :width], hid[rows])

    for copy in w_copies(0, 0):
        copy.wait()
    for i in range(1, slots):
        start_w(i)
        start_x(i)
    wait_x(0)
    for c in range(1, panels):
        for copy in w_copies(0, c):
            copy.wait()
    wait_w(0)
    hide(0)

    @pl.when(live == slots)
    def _():
        for first, end in [(1, min(2, slots)), (2, slots)]:
            for i in range(first, end):
                wait_w(i)
            for i in range(first, end):
                for copy in x_copies(i):
                    copy.wait()
            for i in range(first, end):
                hide(i)
        for i in range(0, slots - 1, 2):
            same = expert_at(i) == expert_at(i + 1)
            two_rows = pl.ds(i * block, 2 * block)
            one_row = pl.ds((i + 1) * block, block)
            other = hid[one_row, :width]
            left = jnp.concatenate(
                [hid[pl.ds(i * block, block), :width], jnp.where(same, other, jnp.zeros_like(other))]
            )
            add_product(expert_at(i), left, hid[two_rows])
        for i in range(0, slots - 1, 2):

            @pl.when(expert_at(i) != expert_at(i + 1))
            def _():
                add_gram(i + 1)

        if slots % 2:
            add_gram(slots - 1)

    @pl.when(live < slots)
    def _():
        for i in range(1, slots - 1):

            @pl.when(i < live)
            def _():
                wait_w(i)
                for copy in x_copies(i):
                    copy.wait()
                hide(i)
                add_gram(i - 1)

        add_gram(live - 1)

    if plan is not None:
        me = lax.axis_index("dp")
        core = lax.rem(me, 2)
        chip = me // 2
        tables = [block_offsets(plan, c) for c in (0, 1)]
        loads = []
        for k in range(len(tables[0])):
            mine = jnp.where(core == 0, tables[0][k], tables[1][k])
            theirs = jnp.where(core == 0, tables[1][k], tables[0][k])
            own[k] = acc[2 * (chip ^ mine) + core]
            there = 2 * (chip ^ theirs) + (1 - core)
            loads.append(lambda there=there: acc[there])
        write_codes(loads, msg)


def grams(teacher, student, experts, count, gate, up, ranks, plan):
    slots = experts.shape[0]
    block = teacher.shape[0] // slots
    depth = teacher.shape[1]
    expert_total, _, width = gate.shape
    two = 2 * width
    rows = expert_total * width // ranks
    panels = width // LANES
    scratch = [
        pltpu.VMEM((slots, 2 * block, depth), jnp.bfloat16),
        pltpu.VMEM((expert_total, panels, depth, 2 * LANES), jnp.bfloat16),
        pltpu.VMEM((slots * block, two), jnp.bfloat16),
        pltpu.SMEM((slots,), jnp.int32),
        pltpu.SMEM((slots,), jnp.int32),
    ]
    sems = [
        pltpu.SemaphoreType.DMA((slots, 2)),
        pltpu.SemaphoreType.DMA((expert_total, panels, 2)),
        pltpu.SemaphoreType.DMA((1,)),
    ]
    if plan is None:
        out_shape = jax.ShapeDtypeStruct((expert_total * width, two), jnp.float32)
    else:
        scratch.append(pltpu.VMEM((ranks, rows, two), jnp.float32))
        out_shape = (
            jax.ShapeDtypeStruct((ranks // 2, rows, two), jnp.float32),
            message_shape(ranks // 2, rows, two),
        )
    hbm = pl.BlockSpec(memory_space=pl.ANY)
    return pl.pallas_call(
        functools.partial(gram_kernel, plan),
        out_shape=out_shape,
        in_specs=[hbm, pl.BlockSpec(memory_space=pltpu.SMEM), hbm, hbm, hbm, hbm],
        scratch_shapes=scratch + sems,
        compiler_params=pltpu.CompilerParams(vmem_limit_bytes=51 << 20),
        name="grams",
    )(pltpu.with_memory_space_constraint(experts, pltpu.HBM), count, *[pltpu.with_memory_space_constraint(a, pltpu.HBM) for a in (teacher, student, gate, up)])


def join_kernel(scaling, radix, parts, own, *rest):
    count, rows, width = own.shape
    panels = width // LANES
    msgs = rest[:parts]
    steps = [read_step(msg) for msg in msgs]

    def total(k):
        return own[k] + sum(
            read_block(msg, k, rows, panels, step) for msg, step in zip(msgs, steps)
        )

    if radix == 1:
        rest[parts][...] = total(0) * scaling
        return
    keep, *sends, held = rest[parts:]
    per = count // radix
    for k in range(per, count):
        held[k - per] = total(k)
    for d, send in enumerate(sends):
        write_codes([lambda k=k: held[k] for k in range(d * per, (d + 1) * per)], send)
    for k in range(per):
        keep[k] = total(k)


def join(own, msgs, radix, scaling):
    count, rows, width = own.shape
    if radix == 1:
        out_shape = jax.ShapeDtypeStruct((rows, width), jnp.float32)
        scratch = []
    else:
        per = count // radix
        out_shape = (
            jax.ShapeDtypeStruct((per, rows, width), jnp.float32),
            *[message_shape(per, rows, width)] * (radix - 1),
        )
        scratch = [pltpu.VMEM((count - per, rows, width), jnp.float32)]
    return pl.pallas_call(
        functools.partial(join_kernel, scaling, radix, len(msgs)),
        out_shape=out_shape,
        scratch_shapes=scratch,
        compiler_params=pltpu.CompilerParams(vmem_limit_bytes=32 << 20),
        name=f"join{count}",
    )(own, *msgs)


def local(teacher, student, experts, count, gate, up):
    ranks = lax.axis_size("dp")
    block = teacher.shape[0] // experts.shape[0]
    scaling = 1.0 / (block * ranks)
    total_rows = gate.shape[0] * gate.shape[2]
    rows = total_rows // ranks
    bits = ranks.bit_length() - 1
    coded = ranks >= 4 and ranks == 1 << bits and rows % 16 == 0 and gate.shape[2] % rows == 0
    if not coded:
        acc = grams(teacher, student, experts, count, gate, up, ranks, None)
        return lax.psum_scatter(acc, "dp", scatter_dimension=0, tiled=True) * scaling
    chip_bits = [1 << i for i in range(bits - 1)]
    orders = [chip_bits, chip_bits[:1] + chip_bits[2:3] + chip_bits[1:2] + chip_bits[3:]]
    plan = [[tuple(bits[i : i + 2]) for i in range(0, len(bits), 2)] for bits in orders]
    own, msg = grams(teacher, student, experts, count, gate, up, ranks, plan)
    msgs = [lax.ppermute(msg, "dp", [(p, p ^ 1) for p in range(ranks)])]
    for pair in zip(*plan):
        own, *msgs = join(own, msgs, 1 << len(pair[0]), scaling)
        reach = [stage_offsets(group, core) for core, group in enumerate(pair)]
        msgs = [
            lax.ppermute(msg, "dp", [(p, p ^ (2 * reach[p % 2][i])) for p in range(ranks)])
            for i, msg in enumerate(msgs)
        ]
    return join(own, msgs, 1, scaling)


def solution(mesh):
    return jax.shard_map(
        local,
        mesh=mesh,
        in_specs=(
            P(("groups", "dp"), None),
            P(("groups", "dp"), None),
            P(("groups", "dp")),
            P(("groups", "dp")),
            P("groups", None, None),
            P("groups", None, None),
        ),
        out_specs=P(("groups", "dp"), None),
        check_vma=False,
    )
```

```python
import functools

import jax
import jax.numpy as jnp
from jax import lax
from jax.experimental import pallas as pl
from jax.experimental.pallas import tpu as pltpu
from jax.sharding import PartitionSpec as P

LANES = 128
TAIL = 16
TOP = 32700.0
LEAST = 2.0**-110


def code_scale(exponent, mantissa):
    return (mantissa * (1.0 / 16384.0)) * jnp.exp2(exponent)


def write_codes(blocks, msg_ref):
    rows, width = blocks[0]().shape
    panels = width // LANES
    top = None
    for load in blocks:
        high = jnp.max(jnp.abs(load()), axis=0, keepdims=True)
        for c in range(panels):
            part = high[:, c * LANES : (c + 1) * LANES]
            top = part if top is None else jnp.maximum(top, part)
    top = jnp.maximum(top, LEAST)
    exponent = jnp.ceil(jnp.log2(top))
    mantissa = jnp.ceil(top * jnp.exp2(-exponent) * 16384.0) + 1.0
    factor = TOP / code_scale(exponent, mantissa)
    for k, load in enumerate(blocks):
        for c in range(panels):
            part = load()[:, c * LANES : (c + 1) * LANES] * factor
            at = (k * panels + c) * rows
            msg_ref[at : at + rows, :] = jnp.round(part).astype(jnp.int32).astype(jnp.int16)
    line = lax.broadcasted_iota(jnp.int32, (TAIL, LANES), 0)
    tail = jnp.where(line == 0, exponent.astype(jnp.int32), mantissa.astype(jnp.int32))
    msg_ref[len(blocks) * panels * rows :, :] = tail.astype(jnp.int16)


def read_step(msg_ref):
    at = msg_ref.shape[0] - TAIL
    tail = msg_ref[at:, :].astype(jnp.int32).astype(jnp.float32)
    return code_scale(tail[0:1], tail[1:2]) * (1.0 / TOP)


def read_block(msg_ref, k, rows, panels, step):
    parts = []
    for c in range(panels):
        at = (k * panels + c) * rows
        parts.append(msg_ref[at : at + rows, :].astype(jnp.int32).astype(jnp.float32) * step)
    return jnp.concatenate(parts, axis=1)


def message_shape(count, rows, width):
    return jax.ShapeDtypeStruct((count * rows * (width // LANES) + TAIL, LANES), jnp.int16)


def block_offsets(plan, core):
    offsets = [0]
    for group in plan[core]:
        offsets = [a ^ b for a in offsets for b in [0, *stage_offsets(group, core)]]
    return offsets


def stage_offsets(group, core):
    if len(group) == 1:
        return list(group)
    one, two = group
    return [one, one | two, two] if core == 0 else [two, one, one | two]


def block_places(plan):
    me = lax.axis_index("dp")
    core = lax.rem(me, 2)
    chip = me // 2
    mine, there = [], []
    for zero, one in zip(block_offsets(plan, 0), block_offsets(plan, 1)):
        mine.append(2 * (chip ^ jnp.where(core == 0, zero, one)) + core)
        there.append(2 * (chip ^ jnp.where(core == 0, one, zero)) + (1 - core))
    return mine, there


def gram_kernel(plan, experts_in, count, teacher, student, gate, up, *rest):
    if plan is None:
        acc, x, w, hid, order, experts, x_sem, w_sem, s_sem = rest
    else:
        acc, msg, x, w, hid, order, experts, x_sem, w_sem, s_sem = rest
    slots, both, _ = x.shape
    block = both // 2
    expert_total, panels, _, pair_width = w.shape
    lanes = pair_width // 2
    width = panels * lanes

    def w_copies(e, c):
        cols = pl.ds(c * lanes, lanes)
        return [
            pltpu.make_async_copy(gate.at[e, :, cols], w.at[e, c, :, pl.ds(0, lanes)], w_sem.at[e, c, 0]),
            pltpu.make_async_copy(up.at[e, :, cols], w.at[e, c, :, pl.ds(lanes, lanes)], w_sem.at[e, c, 1]),
        ]

    scalars = [
        pltpu.make_async_copy(experts_in, experts, s_sem.at[0]),
    ]
    for copy in scalars:
        copy.start()
    for c in range(panels):
        for copy in w_copies(0, c):
            copy.start()
    for copy in scalars:
        copy.wait()
    live = count[0]

    keys = [jnp.where(s < live, experts[s], experts[s] + expert_total) for s in range(slots)]
    for s in range(slots):
        place = jnp.int32(0)
        for t in range(slots):
            if t != s:
                ahead = keys[t] <= keys[s] if t < s else keys[t] < keys[s]
                place = place + ahead.astype(jnp.int32)
        order[place] = s

    def expert_at(i):
        return experts[order[i]]

    def fresh(i):
        new = expert_at(i) != (expert_at(i - 1) if i else 0)
        return (i < live) & new

    def x_copies(i):
        rows = pl.ds(order[i] * block, block)
        return [
            pltpu.make_async_copy(student.at[rows], x.at[i, pl.ds(0, block)], x_sem.at[i, 0]),
            pltpu.make_async_copy(teacher.at[rows], x.at[i, pl.ds(block, block)], x_sem.at[i, 1]),
        ]

    def start_w(i):
        @pl.when(fresh(i))
        def _():
            for c in range(panels):
                for copy in w_copies(expert_at(i), c):
                    copy.start()

    def start_x(i):
        @pl.when(i < live)
        def _():
            for copy in x_copies(i):
                copy.start()

    def wait_w(i):
        @pl.when(fresh(i))
        def _():
            for c in range(panels):
                for copy in w_copies(expert_at(i), c):
                    copy.wait()

    def wait_x(i):
        @pl.when(i < live)
        def _():
            for copy in x_copies(i):
                copy.wait()

    start_x(0)
    start_w(0)
    acc[...] = jnp.zeros_like(acc)

    def hide(i):
        expert = expert_at(i)
        rows = pl.ds(i * block, block)
        for c in range(panels):
            out = jnp.dot(x[i], w[expert, c], preferred_element_type=jnp.float32)
            gate_out = out[:, :lanes]
            part = (gate_out / (1.0 + jnp.exp(-gate_out)) * out[:, lanes:]).astype(jnp.bfloat16)
            hid[rows, c * lanes : (c + 1) * lanes] = part[:block]
            hid[rows, width + c * lanes : width + (c + 1) * lanes] = part[block:]

    def add_product(expert, left, right):
        gram = lax.dot_general(left, right, (((0,), (0,)), ((), ())), preferred_element_type=jnp.float32)
        if plan is None:
            at = pl.ds(expert * width, width)
            acc[at] = acc[at] + gram
        else:
            per = width // acc.shape[1]
            at = pl.ds(expert * per, per)
            acc[at] = acc[at] + gram.reshape(per, *acc.shape[1:])

    def add_gram(i):
        rows = pl.ds(pl.multiple_of(i * block, block), block)
        add_product(expert_at(i), hid[rows, :width], hid[rows])

    for copy in w_copies(0, 0):
        copy.wait()
    for i in range(1, slots):
        start_w(i)
        start_x(i)
    wait_x(0)
    for c in range(1, panels):
        for copy in w_copies(0, c):
            copy.wait()
    wait_w(0)
    hide(0)

    @pl.when(live == slots)
    def _():
        for first, end in [(1, min(2, slots)), (2, slots)]:
            for i in range(first, end):
                wait_w(i)
            for i in range(first, end):
                for copy in x_copies(i):
                    copy.wait()
            for i in range(first, end):
                hide(i)
        for i in range(0, slots - 1, 2):
            same = expert_at(i) == expert_at(i + 1)
            two_rows = pl.ds(i * block, 2 * block)
            one_row = pl.ds((i + 1) * block, block)
            other = hid[one_row, :width]
            left = jnp.concatenate(
                [hid[pl.ds(i * block, block), :width], jnp.where(same, other, jnp.zeros_like(other))]
            )
            add_product(expert_at(i), left, hid[two_rows])
        for i in range(0, slots - 1, 2):

            @pl.when(expert_at(i) != expert_at(i + 1))
            def _():
                add_gram(i + 1)

        if slots % 2:
            add_gram(slots - 1)

    @pl.when(live < slots)
    def _():
        for i in range(1, slots - 1):

            @pl.when(i < live)
            def _():
                wait_w(i)
                for copy in x_copies(i):
                    copy.wait()
                hide(i)
                add_gram(i - 1)

        add_gram(live - 1)

    if plan is not None:
        _, there = block_places(plan)
        loads = [lambda k=k: acc[k] for k in there]
        write_codes(loads, msg)


def grams(teacher, student, experts, count, gate, up, ranks, plan):
    slots = experts.shape[0]
    block = teacher.shape[0] // slots
    depth = teacher.shape[1]
    expert_total, _, width = gate.shape
    two = 2 * width
    rows = expert_total * width // ranks
    panels = width // LANES
    scratch = [
        pltpu.VMEM((slots, 2 * block, depth), jnp.bfloat16),
        pltpu.VMEM((expert_total, panels, depth, 2 * LANES), jnp.bfloat16),
        pltpu.VMEM((slots * block, two), jnp.bfloat16),
        pltpu.SMEM((slots,), jnp.int32),
        pltpu.SMEM((slots,), jnp.int32),
    ]
    sems = [
        pltpu.SemaphoreType.DMA((slots, 2)),
        pltpu.SemaphoreType.DMA((expert_total, panels, 2)),
        pltpu.SemaphoreType.DMA((1,)),
    ]
    if plan is None:
        out_shape = jax.ShapeDtypeStruct((expert_total * width, two), jnp.float32)
    else:
        out_shape = (
            jax.ShapeDtypeStruct((ranks, rows, two), jnp.float32),
            message_shape(ranks // 2, rows, two),
        )
    hbm = pl.BlockSpec(memory_space=pl.ANY)
    return pl.pallas_call(
        functools.partial(gram_kernel, plan),
        out_shape=out_shape,
        in_specs=[hbm, pl.BlockSpec(memory_space=pltpu.SMEM), hbm, hbm, hbm, hbm],
        scratch_shapes=scratch + sems,
        compiler_params=pltpu.CompilerParams(vmem_limit_bytes=49 << 20),
        name="grams",
    )(pltpu.with_memory_space_constraint(experts, pltpu.HBM), count, *[pltpu.with_memory_space_constraint(a, pltpu.HBM) for a in (teacher, student, gate, up)])


def join_kernel(scaling, radix, parts, plan, own, *rest):
    count, rows, width = own.shape
    places = list(range(count))
    if plan is not None:
        places, _ = block_places(plan)
        count = len(places)
    panels = width // LANES
    msgs = rest[:parts]
    steps = [read_step(msg) for msg in msgs]

    def total(k):
        return own[places[k]] + sum(
            read_block(msg, k, rows, panels, step) for msg, step in zip(msgs, steps)
        )

    if radix == 1:
        rest[parts][...] = total(0) * scaling
        return
    keep, *sends, held = rest[parts:]
    per = count // radix
    for k in range(per, count):
        held[k - per] = total(k)
    for d, send in enumerate(sends):
        write_codes([lambda k=k: held[k] for k in range(d * per, (d + 1) * per)], send)
    for k in range(per):
        keep[k] = total(k)


def join(own, msgs, radix, scaling, plan=None):
    count, rows, width = own.shape
    if plan is not None:
        count //= 2
    if radix == 1:
        out_shape = jax.ShapeDtypeStruct((rows, width), jnp.float32)
        scratch = []
    else:
        per = count // radix
        out_shape = (
            jax.ShapeDtypeStruct((per, rows, width), jnp.float32),
            *[message_shape(per, rows, width)] * (radix - 1),
        )
        scratch = [pltpu.VMEM((count - per, rows, width), jnp.float32)]
    return pl.pallas_call(
        functools.partial(join_kernel, scaling, radix, len(msgs), plan),
        out_shape=out_shape,
        scratch_shapes=scratch,
        compiler_params=pltpu.CompilerParams(vmem_limit_bytes=32 << 20),
        name=f"join{count}",
    )(own, *msgs)


def local(teacher, student, experts, count, gate, up):
    ranks = lax.axis_size("dp")
    block = teacher.shape[0] // experts.shape[0]
    scaling = 1.0 / (block * ranks)
    total_rows = gate.shape[0] * gate.shape[2]
    rows = total_rows // ranks
    bits = ranks.bit_length() - 1
    coded = ranks >= 4 and ranks == 1 << bits and rows % 16 == 0 and gate.shape[2] % rows == 0
    if not coded:
        acc = grams(teacher, student, experts, count, gate, up, ranks, None)
        return lax.psum_scatter(acc, "dp", scatter_dimension=0, tiled=True) * scaling
    chip_bits = [1 << i for i in range(bits - 1)]
    orders = [chip_bits, chip_bits[:1] + chip_bits[2:3] + chip_bits[1:2] + chip_bits[3:]]
    plan = [[tuple(bits[i : i + 2]) for i in range(0, len(bits), 2)] for bits in orders]
    own, msg = grams(teacher, student, experts, count, gate, up, ranks, plan)
    msgs = [lax.ppermute(msg, "dp", [(p, p ^ 1) for p in range(ranks)])]
    for stage, pair in enumerate(zip(*plan)):
        own, *msgs = join(own, msgs, 1 << len(pair[0]), scaling, None if stage else plan)
        reach = [stage_offsets(group, core) for core, group in enumerate(pair)]
        msgs = [
            lax.ppermute(msg, "dp", [(p, p ^ (2 * reach[p % 2][i])) for p in range(ranks)])
            for i, msg in enumerate(msgs)
        ]
    return join(own, msgs, 1, scaling)


def solution(mesh):
    return jax.shard_map(
        local,
        mesh=mesh,
        in_specs=(
            P(("groups", "dp"), None),
            P(("groups", "dp"), None),
            P(("groups", "dp")),
            P(("groups", "dp")),
            P("groups", None, None),
            P("groups", None, None),
        ),
        out_specs=P(("groups", "dp"), None),
        check_vma=False,
    )
```

```python
import functools

import jax
import jax.numpy as jnp
from jax import lax
from jax.experimental import pallas as pl
from jax.experimental.pallas import tpu as pltpu
from jax.sharding import PartitionSpec as P

LANES = 128
TAIL = 16
TOP = 32700.0
LEAST = 2.0**-110


def code_scale(exponent, mantissa):
    return (mantissa * (1.0 / 16384.0)) * jnp.exp2(exponent)


def write_codes(blocks, msg_ref):
    rows, width = blocks[0]().shape
    panels = width // LANES
    top = None
    for load in blocks:
        high = jnp.max(jnp.abs(load()), axis=0, keepdims=True)
        for c in range(panels):
            part = high[:, c * LANES : (c + 1) * LANES]
            top = part if top is None else jnp.maximum(top, part)
    top = jnp.maximum(top, LEAST)
    exponent = jnp.ceil(jnp.log2(top))
    mantissa = jnp.ceil(top * jnp.exp2(-exponent) * 16384.0) + 1.0
    factor = TOP / code_scale(exponent, mantissa)
    for k, load in enumerate(blocks):
        for c in range(panels):
            part = load()[:, c * LANES : (c + 1) * LANES] * factor
            at = (k * panels + c) * rows
            msg_ref[at : at + rows, :] = jnp.round(part).astype(jnp.int32).astype(jnp.int16)
    line = lax.broadcasted_iota(jnp.int32, (TAIL, LANES), 0)
    tail = jnp.where(line == 0, exponent.astype(jnp.int32), mantissa.astype(jnp.int32))
    msg_ref[len(blocks) * panels * rows :, :] = tail.astype(jnp.int16)


def read_step(msg_ref):
    at = msg_ref.shape[0] - TAIL
    tail = msg_ref[at:, :].astype(jnp.int32).astype(jnp.float32)
    return code_scale(tail[0:1], tail[1:2]) * (1.0 / TOP)


def read_block(msg_ref, k, rows, panels, step):
    parts = []
    for c in range(panels):
        at = (k * panels + c) * rows
        parts.append(msg_ref[at : at + rows, :].astype(jnp.int32).astype(jnp.float32) * step)
    return jnp.concatenate(parts, axis=1)


def message_shape(count, rows, width):
    return jax.ShapeDtypeStruct((count * rows * (width // LANES) + TAIL, LANES), jnp.int16)


def block_offsets(plan, core):
    offsets = [0]
    for group in plan[core]:
        offsets = [a ^ b for a in offsets for b in [0, *stage_offsets(group, core)]]
    return offsets


def stage_offsets(group, core):
    if len(group) == 1:
        return list(group)
    one, two = group
    return [one, one | two, two] if core == 0 else [two, one, one | two]


def gram_kernel(plan, experts_in, count, teacher, student, gate, up, *rest):
    if plan is None:
        acc, x, w, hid, order, experts, x_sem, w_sem, s_sem = rest
    else:
        own, msg, x, w, hid, order, experts, acc, x_sem, w_sem, s_sem = rest
    slots, both, _ = x.shape
    block = both // 2
    expert_total, panels, _, pair_width = w.shape
    lanes = pair_width // 2
    width = panels * lanes

    def w_copies(e, c):
        cols = pl.ds(c * lanes, lanes)
        return [
            pltpu.make_async_copy(gate.at[e, :, cols], w.at[e, c, :, pl.ds(0, lanes)], w_sem.at[e, c, 0]),
            pltpu.make_async_copy(up.at[e, :, cols], w.at[e, c, :, pl.ds(lanes, lanes)], w_sem.at[e, c, 1]),
        ]

    scalars = [
        pltpu.make_async_copy(experts_in, experts, s_sem.at[0]),
    ]
    for copy in scalars:
        copy.start()
    for c in range(panels):
        for copy in w_copies(0, c):
            copy.start()
    for copy in scalars:
        copy.wait()
    live = count[0]

    keys = [jnp.where(s < live, experts[s], experts[s] + expert_total) for s in range(slots)]
    for s in range(slots):
        place = jnp.int32(0)
        for t in range(slots):
            if t != s:
                ahead = keys[t] <= keys[s] if t < s else keys[t] < keys[s]
                place = place + ahead.astype(jnp.int32)
        order[place] = s

    def expert_at(i):
        return experts[order[i]]

    def fresh(i):
        new = expert_at(i) != (expert_at(i - 1) if i else 0)
        return (i < live) & new

    def x_copies(i):
        rows = pl.ds(order[i] * block, block)
        return [
            pltpu.make_async_copy(student.at[rows], x.at[i, pl.ds(0, block)], x_sem.at[i, 0]),
            pltpu.make_async_copy(teacher.at[rows], x.at[i, pl.ds(block, block)], x_sem.at[i, 1]),
        ]

    def start_w(i):
        @pl.when(fresh(i))
        def _():
            for c in range(panels):
                for copy in w_copies(expert_at(i), c):
                    copy.start()

    def start_x(i):
        @pl.when(i < live)
        def _():
            for copy in x_copies(i):
                copy.start()

    def wait_w(i):
        @pl.when(fresh(i))
        def _():
            for c in range(panels):
                for copy in w_copies(expert_at(i), c):
                    copy.wait()

    def wait_x(i):
        @pl.when(i < live)
        def _():
            for copy in x_copies(i):
                copy.wait()

    start_x(0)
    start_w(0)
    acc[...] = jnp.zeros_like(acc)

    def hide(i):
        expert = expert_at(i)
        rows = pl.ds(i * block, block)
        for c in range(panels):
            out = jnp.dot(x[i], w[expert, c], preferred_element_type=jnp.float32)
            gate_out = out[:, :lanes]
            part = (gate_out / (1.0 + jnp.exp(-gate_out)) * out[:, lanes:]).astype(jnp.bfloat16)
            hid[rows, c * lanes : (c + 1) * lanes] = part[:block]
            hid[rows, width + c * lanes : width + (c + 1) * lanes] = part[block:]

    def add_product(expert, left, right):
        gram = lax.dot_general(left, right, (((0,), (0,)), ((), ())), preferred_element_type=jnp.float32)
        if plan is None:
            at = pl.ds(expert * width, width)
            acc[at] = acc[at] + gram
        else:
            per = width // acc.shape[1]
            at = pl.ds(expert * per, per)
            acc[at] = acc[at] + gram.reshape(per, *acc.shape[1:])

    def add_gram(i):
        rows = pl.ds(pl.multiple_of(i * block, block), block)
        add_product(expert_at(i), hid[rows, :width], hid[rows])

    for copy in w_copies(0, 0):
        copy.wait()
    for i in range(1, slots):
        start_w(i)
        start_x(i)
    wait_x(0)
    for c in range(1, panels):
        for copy in w_copies(0, c):
            copy.wait()
    wait_w(0)
    hide(0)

    @pl.when(live == slots)
    def _():
        for first, end in [(1, max(1, slots // 2)), (max(1, slots // 2), slots)]:
            for i in range(first, end):
                wait_w(i)
            for i in range(first, end):
                for copy in x_copies(i):
                    copy.wait()
            for i in range(first, end):
                hide(i)
        for i in range(0, slots - 1, 2):
            same = expert_at(i) == expert_at(i + 1)
            two_rows = pl.ds(i * block, 2 * block)
            one_row = pl.ds((i + 1) * block, block)
            other = hid[one_row, :width]
            left = jnp.concatenate(
                [hid[pl.ds(i * block, block), :width], jnp.where(same, other, jnp.zeros_like(other))]
            )
            add_product(expert_at(i), left, hid[two_rows])
        for i in range(0, slots - 1, 2):

            @pl.when(expert_at(i) != expert_at(i + 1))
            def _():
                add_gram(i + 1)

        if slots % 2:
            add_gram(slots - 1)

    @pl.when(live < slots)
    def _():
        for i in range(1, slots - 1):

            @pl.when(i < live)
            def _():
                wait_w(i)
                for copy in x_copies(i):
                    copy.wait()
                hide(i)
                add_gram(i - 1)

        add_gram(live - 1)

    if plan is not None:
        me = lax.axis_index("dp")
        core = lax.rem(me, 2)
        chip = me // 2
        tables = [block_offsets(plan, c) for c in (0, 1)]
        loads = []
        for k in range(len(tables[0])):
            mine = jnp.where(core == 0, tables[0][k], tables[1][k])
            theirs = jnp.where(core == 0, tables[1][k], tables[0][k])
            own[k] = acc[2 * (chip ^ mine) + core]
            there = 2 * (chip ^ theirs) + (1 - core)
            loads.append(lambda there=there: acc[there])
        write_codes(loads, msg)


def grams(teacher, student, experts, count, gate, up, ranks, plan):
    slots = experts.shape[0]
    block = teacher.shape[0] // slots
    depth = teacher.shape[1]
    expert_total, _, width = gate.shape
    two = 2 * width
    rows = expert_total * width // ranks
    panels = width // LANES
    scratch = [
        pltpu.VMEM((slots, 2 * block, depth), jnp.bfloat16),
        pltpu.VMEM((expert_total, panels, depth, 2 * LANES), jnp.bfloat16),
        pltpu.VMEM((slots * block, two), jnp.bfloat16),
        pltpu.SMEM((slots,), jnp.int32),
        pltpu.SMEM((slots,), jnp.int32),
    ]
    sems = [
        pltpu.SemaphoreType.DMA((slots, 2)),
        pltpu.SemaphoreType.DMA((expert_total, panels, 2)),
        pltpu.SemaphoreType.DMA((1,)),
    ]
    if plan is None:
        out_shape = jax.ShapeDtypeStruct((expert_total * width, two), jnp.float32)
    else:
        scratch.append(pltpu.VMEM((ranks, rows, two), jnp.float32))
        out_shape = (
            jax.ShapeDtypeStruct((ranks // 2, rows, two), jnp.float32),
            message_shape(ranks // 2, rows, two),
        )
    hbm = pl.BlockSpec(memory_space=pl.ANY)
    return pl.pallas_call(
        functools.partial(gram_kernel, plan),
        out_shape=out_shape,
        in_specs=[hbm, pl.BlockSpec(memory_space=pltpu.SMEM), hbm, hbm, hbm, hbm],
        scratch_shapes=scratch + sems,
        compiler_params=pltpu.CompilerParams(vmem_limit_bytes=51 << 20),
        name="grams",
    )(pltpu.with_memory_space_constraint(experts, pltpu.HBM), count, *[pltpu.with_memory_space_constraint(a, pltpu.HBM) for a in (teacher, student, gate, up)])


def join_kernel(scaling, radix, parts, own, *rest):
    count, rows, width = own.shape
    panels = width // LANES
    msgs = rest[:parts]
    steps = [read_step(msg) for msg in msgs]

    def total(k):
        return own[k] + sum(
            read_block(msg, k, rows, panels, step) for msg, step in zip(msgs, steps)
        )

    if radix == 1:
        rest[parts][...] = total(0) * scaling
        return
    keep, *sends, held = rest[parts:]
    per = count // radix
    for k in range(per, count):
        held[k - per] = total(k)
    for d, send in enumerate(sends):
        write_codes([lambda k=k: held[k] for k in range(d * per, (d + 1) * per)], send)
    for k in range(per):
        keep[k] = total(k)


def join(own, msgs, radix, scaling):
    count, rows, width = own.shape
    if radix == 1:
        out_shape = jax.ShapeDtypeStruct((rows, width), jnp.float32)
        scratch = []
    else:
        per = count // radix
        out_shape = (
            jax.ShapeDtypeStruct((per, rows, width), jnp.float32),
            *[message_shape(per, rows, width)] * (radix - 1),
        )
        scratch = [pltpu.VMEM((count - per, rows, width), jnp.float32)]
    return pl.pallas_call(
        functools.partial(join_kernel, scaling, radix, len(msgs)),
        out_shape=out_shape,
        scratch_shapes=scratch,
        compiler_params=pltpu.CompilerParams(vmem_limit_bytes=32 << 20),
        name=f"join{count}",
    )(own, *msgs)


def local(teacher, student, experts, count, gate, up):
    ranks = lax.axis_size("dp")
    block = teacher.shape[0] // experts.shape[0]
    scaling = 1.0 / (block * ranks)
    total_rows = gate.shape[0] * gate.shape[2]
    rows = total_rows // ranks
    bits = ranks.bit_length() - 1
    coded = ranks >= 4 and ranks == 1 << bits and rows % 16 == 0 and gate.shape[2] % rows == 0
    if not coded:
        acc = grams(teacher, student, experts, count, gate, up, ranks, None)
        return lax.psum_scatter(acc, "dp", scatter_dimension=0, tiled=True) * scaling
    chip_bits = [1 << i for i in range(bits - 1)]
    orders = [chip_bits, chip_bits[:1] + chip_bits[2:3] + chip_bits[1:2] + chip_bits[3:]]
    plan = [[tuple(bits[i : i + 2]) for i in range(0, len(bits), 2)] for bits in orders]
    own, msg = grams(teacher, student, experts, count, gate, up, ranks, plan)
    msgs = [lax.ppermute(msg, "dp", [(p, p ^ 1) for p in range(ranks)])]
    for pair in zip(*plan):
        own, *msgs = join(own, msgs, 1 << len(pair[0]), scaling)
        reach = [stage_offsets(group, core) for core, group in enumerate(pair)]
        msgs = [
            lax.ppermute(msg, "dp", [(p, p ^ (2 * reach[p % 2][i])) for p in range(ranks)])
            for i, msg in enumerate(msgs)
        ]
    return join(own, msgs, 1, scaling)


def solution(mesh):
    return jax.shard_map(
        local,
        mesh=mesh,
        in_specs=(
            P(("groups", "dp"), None),
            P(("groups", "dp"), None),
            P(("groups", "dp")),
            P(("groups", "dp")),
            P("groups", None, None),
            P("groups", None, None),
        ),
        out_specs=P(("groups", "dp"), None),
        check_vma=False,
    )
```
